128 devices in a mesh: row: 8 (over y, x_lo), col: 16 (over z, x_hi, core).
Axes of the slice: x: 4 (x_hi: 2, x_lo: 2; x = x_hi * 2 + x_lo), y: 4, z: 4, core: 2. Of those that a mesh axis runs over, the one named last changes fastest.
Arguments:
- inputs: bfloat16 [1024, 8192], P('row', 'col'), may hold values from -6 to 6
- out_grad: bfloat16 [1024, 8192], P('row', 'col'), may hold values from -6 to 6
- gain: float32 [8192], P('col'), may hold values from 0.1 to 1.9
- w_gate: bfloat16 [8192, 28672], P('col', 'row'), may hold values from -0.0625 to 0.0625
- w_up: bfloat16 [8192, 28672], P('col', 'row'), may hold values from -0.0625 to 0.0625
- w_down: bfloat16 [28672, 8192], P('row', 'col'), may hold values from -0.03125 to 0.03125
- gate_pre: bfloat16 [1024, 28672], P('col', 'row'), may hold values from -8 to 8
- up_pre: bfloat16 [1024, 28672], P('col', 'row'), may hold values from -6 to 6
Outputs:
- d_input: bfloat16 [1024, 8192], P('row', 'col')
- grad_gain: float32 [8192], P('col')
- grad_gate: bfloat16 [8192, 28672], P('col', 'row')
- grad_up: bfloat16 [8192, 28672], P('col', 'row')
- grad_down: bfloat16 [28672, 8192], P('row', 'col')
The draws below stay inside these ranges and needn't reach their ends.
All inputs are finite; a program needn't handle non-finite values.
Results may differ from the reference program's by a relative error of at most 0.0058.
Values may be sent and summed in bfloat16 or wider, within the bound.
No kernel may reach another device: no remote copies, remote signals or barrier semaphores. Data moves between devices by JAX's collectives and lax.ppermute only.
A program may use at most 128 MiB of HBM per device.

```python
import jax
import jax.numpy as jnp
from jax import lax

D = 8192
FF = 28672
TOKENS = 1024


def block_levels(rng, shape, shards, smallest, top_value):
    level, own = 1.0, jax.random.fold_in(rng, 6)
    for dim, shards_of in shards:
        steps = jnp.exp(jax.random.uniform(jax.random.fold_in(own, dim), (shards_of,), jnp.float32, smallest / len(shards), top_value / len(shards)))
        level = level * jnp.repeat(steps, shape[dim] // shards_of).reshape([-1 if axis == dim else 1 for axis in range(len(shape))])
    return level


def gaussian(own_key, dims, width, reach, cuts=(), kind=jnp.bfloat16):
    level = block_levels(own_key, dims, cuts, -0.22, 0.18) if cuts else 1.0
    drawn = jax.random.normal(own_key, dims, jnp.float32) * width * level
    return jnp.minimum(jnp.maximum(drawn, -reach), reach).astype(kind)


def setup_inputs(seed: int = 0) -> dict:
    streams_of = jax.random.split(jax.random.key(seed), 9)
    return {
        "inputs": gaussian(streams_of[0], (TOKENS, D), 1.0, 6.0, ((0, 8), (1, 16))),
        "out_grad": gaussian(streams_of[1], (TOKENS, D), 1.0, 6.0, ((0, 8), (1, 16))),
        "gain": jnp.clip(1.0 + 0.18 * jax.random.normal(streams_of[2], (D,), jnp.float32), 0.1, 1.9),
        "w_gate": gaussian(streams_of[3], (D, FF), D ** -0.5, 0.0625, ((0, 16), (1, 8))),
        "w_up": gaussian(streams_of[4], (D, FF), D ** -0.5, 0.0625, ((0, 16), (1, 8))),
        "w_down": gaussian(streams_of[5], (FF, D), FF ** -0.5, 0.03125, ((0, 8), (1, 16))),
        "gate_pre": gaussian(streams_of[6], (TOKENS, FF), 1.5, 8.0, ((0, 16), (1, 8))),
        "up_pre": gaussian(streams_of[7], (TOKENS, FF), 1.0, 6.0, ((0, 16), (1, 8))),
    }


EPS = 1e-05

def contract_rows(left, right):
    return lax.dot_general(left, right, (((0,), (0,)), ((), ())), preferred_element_type=jnp.float32)

def contract_cols(left, right):
    return lax.dot_general(left, right, (((1,), (1,)), ((), ())), preferred_element_type=jnp.float32)

def reference(inputs, out_grad, gain, w_gate, w_up, w_down, gate_pre, up_pre):
    values = inputs.astype(jnp.float32)
    squares = lax.optimization_barrier(jnp.sum(values * values, axis=1))
    rstd = lax.rsqrt(squares / D + EPS)
    normed = (values * rstd[:, None] * gain[None, :]).astype(jnp.bfloat16)
    d_hidden = contract_cols(out_grad, w_down)
    gates = gate_pre.astype(jnp.float32)
    ups = up_pre.astype(jnp.float32)
    sig = jax.nn.sigmoid(gates)
    silu = gates * sig
    hidden = (silu * ups).astype(jnp.bfloat16)
    d_gate = (d_hidden * ups * sig * (1.0 + gates * (1.0 - sig))).astype(jnp.bfloat16)
    d_up = (d_hidden * silu).astype(jnp.bfloat16)
    grad_down = contract_rows(hidden, out_grad).astype(jnp.bfloat16)
    grad_gate = contract_rows(normed, d_gate).astype(jnp.bfloat16)
    grad_up = contract_rows(normed, d_up).astype(jnp.bfloat16)
    d_normed = contract_cols(d_gate, w_gate) + contract_cols(d_up, w_up)
    grad_gain = lax.optimization_barrier(jnp.sum(d_normed * values * rstd[:, None], axis=0))
    proj = lax.optimization_barrier(jnp.sum(d_normed * gain[None, :] * values, axis=1))
    scaled = rstd * rstd * rstd * proj / D
    d_input = (out_grad.astype(jnp.float32) + rstd[:, None] * d_normed * gain[None, :] - values * scaled[:, None]).astype(jnp.bfloat16)
    return (d_input, grad_gain, grad_gate, grad_up, grad_down)
```

```python
import jax
import jax.numpy as jnp
from jax import lax
from jax.sharding import PartitionSpec as P

EPS = 1e-05
NZ, NX, NC = 4, 2, 2
NY, NL = 4, 2
PARTS = 2
F32, BF16 = jnp.float32, jnp.bfloat16


def contract_rows(left, right):
    return lax.dot_general(left, right, (((0,), (0,)), ((), ())), preferred_element_type=F32)


def contract_cols(left, right):
    return lax.dot_general(left, right, (((1,), (1,)), ((), ())), preferred_element_type=F32)


def col_to(x, dz=0, dx=0, dc=0):
    pairs = []
    for z in range(NZ):
        for h in range(NX):
            for c in range(NC):
                dst = (((z + dz) % NZ) * NX + (h + dx) % NX) * NC + (c + dc) % NC
                pairs.append(((z * NX + h) * NC + c, dst))
    return lax.ppermute(x, "col", pairs)


def row_to(x, dy=0, dl=0):
    pairs = []
    for y in range(NY):
        for l in range(NL):
            pairs.append((y * NL + l, ((y + dy) % NY) * NL + (l + dl) % NL))
    return lax.ppermute(x, "row", pairs)


def col_sum(x):
    x = x + col_to(x, dc=1)
    x = x + col_to(x, dx=1)
    flip = lambda v: v ^ NC * NX
    x = x + lax.ppermute(x, "col", [(i, flip(i)) for i in range(NZ * NX * NC)])
    return x + col_to(x, dz=2)


def row_sum(x):
    x = x + row_to(x, dl=1)
    x = x + lax.ppermute(x, "row", [(i, i ^ NL) for i in range(NY * NL)])
    return x + row_to(x, dy=2)


def gather_chips(block):
    other = col_to(block, dx=1)
    pair = jnp.concatenate([block, other], axis=0)
    below = col_to(pair, dz=1)
    above = col_to(pair, dz=-1)
    t = block.shape[0]
    far0 = col_to(below[:t], dz=1)
    far1 = col_to(above[t:], dz=-1)
    return pair, above, far0, far1, below


def gather_cols(block):
    mine = gather_chips(block)
    theirs = [col_to(piece, dc=1) for piece in mine]
    return jnp.concatenate(list(mine) + theirs, axis=0)


def local(inputs, out_grad, gain, w_gate, w_up, w_down, gate_pre, up_pre):
    rows, feats = inputs.shape
    width = gate_pre.shape[1]
    tok = gate_pre.shape[0]
    total_feats = feats * NZ * NX * NC
    col, row = lax.axis_index("col"), lax.axis_index("row")
    z, h, c = col // (NX * NC), (col // NC) % NX, col % NC
    y, l = row // NL, row % NL

    def place(ky, kl):
        return (((y + ky - z) % NZ) * NX + ((l + kl + h) % NX)) * rows

    def own_first(x):
        a, b = x[:tok], x[tok:]
        return jnp.where(c == 0, x, jnp.concatenate([b, a], axis=0))

    def gather_rows(x):
        x = own_first(x)
        full = jnp.zeros((rows * NY * NL, x.shape[1]), x.dtype)
        for ky in range(NY):
            for kl in range(NL):
                piece = row_to(x, -ky, kl) if ky or kl else x
                full = lax.dynamic_update_slice(full, piece, (place(ky, kl), 0))
        full = full.reshape(NZ * NX, NC, tok, x.shape[1])
        return full[:, 0].reshape(-1, x.shape[1]), full[:, 1].reshape(-1, x.shape[1])

    w_down_other = col_to(w_down, dc=1)
    gates = gate_pre.astype(F32)
    ups = up_pre.astype(F32)
    sig = jax.nn.sigmoid(gates)
    silu = gates * sig
    hidden = (silu * ups).astype(BF16)

    out_mine, out_theirs = gather_rows(out_grad)
    out_other = col_to(out_theirs, dc=1)
    hidden_all = gather_cols(hidden)

    step = NX * tok
    partial = {}
    for k in (2, 1, 3, 0):
        cut = slice(k * step, (k + 1) * step)
        partial[k] = contract_cols(out_mine[cut], w_down) + contract_cols(out_other[cut], w_down_other)
    d_hidden = partial[0][:tok]
    for k in (2, 1, 3, 0):
        for j in range(NX):
            if k or j:
                sent = col_to(partial[k][j * tok:(j + 1) * tok].astype(BF16), dz=k, dx=j)
                d_hidden = d_hidden + sent.astype(F32)
    d_gate = (d_hidden * ups * sig * (1.0 + gates * (1.0 - sig))).astype(BF16)
    d_up = (d_hidden * silu).astype(BF16)
    gate_all = gather_cols(d_gate)
    up_all = gather_cols(d_up)

    values = inputs.astype(F32)
    squares = col_sum(jnp.sum(values * values, axis=1).reshape(1, rows)).reshape(rows)
    rstd = lax.rsqrt(squares / total_feats + EPS)
    normed = (values * rstd[:, None] * gain[None, :]).astype(BF16)
    normed_all = jnp.concatenate(gather_rows(normed), axis=0)
    out_all = jnp.concatenate([out_mine, out_theirs], axis=0)

    term = contract_cols(gate_all, w_gate) + contract_cols(up_all, w_up)
    term = term.reshape(NC, NZ * NX, tok, feats).transpose(1, 0, 2, 3).reshape(-1, feats)
    d_normed = lax.dynamic_slice(term, (place(0, 0), 0), (rows, feats))
    for ky in range(NY):
        for kl in range(NL):
            if ky or kl:
                piece = lax.dynamic_slice(term, (place(ky, kl), 0), (rows, feats))
                d_normed = d_normed + row_to(piece.astype(BF16), ky, kl).astype(F32)
    d_normed = own_first(d_normed)

    grad_down = contract_rows(hidden_all, out_all).astype(BF16)
    grad_gate = contract_rows(normed_all, gate_all).astype(BF16)
    grad_up = contract_rows(normed_all, up_all).astype(BF16)
    grad_gain = row_sum(jnp.sum(d_normed * values * rstd[:, None], axis=0).reshape(1, feats)).reshape(feats)
    proj = col_sum(jnp.sum(d_normed * gain[None, :] * values, axis=1).reshape(1, rows)).reshape(rows)
    scaled = rstd * rstd * rstd * proj / total_feats
    d_input = (
        out_grad.astype(F32) + rstd[:, None] * d_normed * gain[None, :] - values * scaled[:, None]
    ).astype(BF16)
    return (d_input, grad_gain, grad_gate, grad_up, grad_down)


def solution(mesh):
    in_specs = (
        P("row", "col"),
        P("row", "col"),
        P("col"),
        P("col", "row"),
        P("col", "row"),
        P("row", "col"),
        P("col", "row"),
        P("col", "row"),
    )
    out_specs = (P("row", "col"), P("col"), P("col", "row"), P("col", "row"), P("row", "col"))
    return jax.shard_map(local, mesh=mesh, in_specs=in_specs, out_specs=out_specs, check_vma=False)
```

```python
import jax
import jax.numpy as jnp
from jax import lax
from jax.experimental import pallas as pl
from jax.experimental.pallas import tpu as pltpu
from jax.sharding import PartitionSpec as P

EPS = 1e-05
NZ, NX, NC = 4, 2, 2
NY, NL = 4, 2
F32, BF16 = jnp.float32, jnp.bfloat16


def dot(left, right, a, b):
    return lax.dot_general(left, right, (((a,), (b,)), ((), ())), preferred_element_type=F32)


def kernel_call(body, name, steps, in_specs, out_specs, out_shape, scratch, args):
    return pl.pallas_call(
        body,
        grid=(steps,),
        in_specs=in_specs,
        out_specs=out_specs,
        out_shape=out_shape,
        scratch_shapes=scratch,
        compiler_params=pltpu.CompilerParams(vmem_limit_bytes=60 * 2**20),
        name=name,
    )(*args)


def hidden_units(left, left_other, w, w_other, steps):
    m, f = left.shape
    width = w.shape[0]
    n = width // steps

    def body(l, lo, w, wo, out):
        out[...] = dot(l[...], w[...], 1, 1) + dot(lo[...], wo[...], 1, 1)

    lefts = [pl.BlockSpec((m, f), lambda i: (0, 0))] * 2
    rights = [pl.BlockSpec((n, f), lambda i: (i, 0))] * 2
    return kernel_call(
        body, "hidden_units", steps, lefts + rights, pl.BlockSpec((m, n), lambda i: (0, i)),
        jax.ShapeDtypeStruct((m, width), F32), [], (left, left_other, w, w_other),
    )


def input_grads(pieces, w_gate, w_up, steps):
    f, width = w_gate.shape
    tok, k, count = pieces[0].shape[0] // 2, width // steps, len(pieces)

    def body(*refs):
        parts, (wg, wu, out) = refs[:count], refs[count:]
        gate = jnp.concatenate([p[:tok] for p in parts], axis=0)
        up = jnp.concatenate([p[tok:] for p in parts], axis=0)
        total = dot(gate, wg[...], 1, 1) + dot(up, wu[...], 1, 1)

        @pl.when(pl.program_id(0) == 0)
        def _():
            out[...] = total

        @pl.when(pl.program_id(0) > 0)
        def _():
            out[...] += total

    specs = [pl.BlockSpec((2 * tok, k), lambda i: (0, i))] * count + [pl.BlockSpec((f, k), lambda i: (0, i))] * 2
    m = tok * count
    return kernel_call(
        body, "input_grads", steps, specs, pl.BlockSpec((m, f), lambda i: (0, 0)),
        jax.ShapeDtypeStruct((m, f), F32), [], (*pieces, w_gate, w_up),
    )


def gate_up_grads(normed_t, pieces, steps):
    f, t = normed_t.shape
    tok, width, count = pieces[0].shape[0] // 2, pieces[0].shape[1], len(pieces)
    n = width // steps

    def body(left, *refs):
        parts, (gate_out, up_out) = refs[:count], refs[count:]
        left = left[...]
        gate_out[...] = dot(left, jnp.concatenate([p[:tok] for p in parts], axis=0), 1, 0).astype(BF16)
        up_out[...] = dot(left, jnp.concatenate([p[tok:] for p in parts], axis=0), 1, 0).astype(BF16)

    specs = [pl.BlockSpec((f, t), lambda i: (0, 0))] + [pl.BlockSpec((2 * tok, n), lambda i: (0, i))] * count
    return kernel_call(
        body, "gate_up_grads", steps, specs, [pl.BlockSpec((f, n), lambda i: (0, i))] * 2,
        [jax.ShapeDtypeStruct((f, width), BF16)] * 2, [], (normed_t, *pieces),
    )


def down_grads(hid, hid_other, out, steps):
    f, (t, width) = out.shape[1], hid.shape
    n = width // steps

    def body(left, left_other, right, total):
        total[...] = (dot(left[...], right[:t], 0, 0) + dot(left_other[...], right[t:], 0, 0)).astype(BF16)

    specs = [pl.BlockSpec((t, n), lambda i: (0, i))] * 2 + [pl.BlockSpec((2 * t, f), lambda i: (0, 0))]
    return kernel_call(
        body, "down_grads", steps, specs, pl.BlockSpec((n, f), lambda i: (i, 0)),
        jax.ShapeDtypeStruct((width, f), BF16), [], (hid, hid_other, out),
    )


def col_to(x, name, dz=0, dx=0, dc=0):
    pairs = []
    for z in range(NZ):
        for h in range(NX):
            for c in range(NC):
                dst = (((z + dz) % NZ) * NX + (h + dx) % NX) * NC + (c + dc) % NC
                pairs.append(((z * NX + h) * NC + c, dst))
    with jax.named_scope(name):
        return lax.ppermute(x, "col", pairs)


def row_to(x, name, dy=0, dl=0):
    pairs = []
    for y in range(NY):
        for l in range(NL):
            pairs.append((y * NL + l, ((y + dy) % NY) * NL + (l + dl) % NL))
    with jax.named_scope(name):
        return lax.ppermute(x, "row", pairs)


def phase(*arrays):
    return lax.optimization_barrier(arrays)


def local(inputs, out_grad, gain, w_gate, w_up, w_down, gate_pre, up_pre):
    rows, feats = inputs.shape
    width = gate_pre.shape[1]
    tok = gate_pre.shape[0]
    half = tok // 2
    total_feats = feats * NZ * NX * NC
    halves = width // 2 if width // 2 % 128 == 0 else width
    steps = width // halves
    col, row = lax.axis_index("col"), lax.axis_index("row")
    z, h, c = col // (NX * NC), (col // NC) % NX, col % NC
    y, l = row // NL, row % NL

    same = (l + h) % NX == 0

    def order(mine, other):
        f = mine.shape[1]
        mine, other = mine.reshape(NC, tok, f), other.reshape(NC, tok, f)
        pair = jnp.stack([jnp.where(same, mine, other), jnp.where(same, other, mine)])
        return jnp.where(c == 0, pair, pair[:, ::-1])[:, :, None]

    def assemble(pairs):
        full = jnp.zeros((NX, NC, NZ, *pairs[0].shape[3:]), pairs[0].dtype)
        for ky, pair in enumerate(pairs):
            full = lax.dynamic_update_slice(full, pair, (0, 0, (y + ky - z) % NZ, 0, 0))
        return full

    def swap(pieces, name):
        return [col_to(piece, name, dc=1) for piece in pieces]

    def neighbour(x, name):
        with jax.named_scope(name):
            return lax.ppermute(x, "col", [(i, i ^ NC * NX) for i in range(NZ * NX * NC)])

    def neighbour_row(x, name):
        with jax.named_scope(name):
            return lax.ppermute(x, "row", [(i, i ^ NL) for i in range(NY * NL)])

    def gather_hidden(x, name):
        groups = [[chip * NC + core for chip in range(NZ * NX)] for core in range(NC)]
        copies = jnp.broadcast_to(x[None], (NZ * NX, *x.shape))
        with jax.named_scope(name):
            return lax.all_to_all(copies, "col", 0, 0, axis_index_groups=groups, tiled=True).reshape(-1, x.shape[1])

    out_xl = row_to(out_grad, "out_xl", dl=1)
    w_down_other = col_to(w_down, "w_down", dc=1)
    gates = gate_pre.astype(F32)
    ups = up_pre.astype(F32)
    sig = jax.nn.sigmoid(gates)
    hidden = (gates * sig * ups).astype(BF16)
    hidden_a, hidden_b = hidden[:, :halves], hidden[:, halves:]
    pair = order(out_grad, out_xl)
    pair, hidden_a, hidden_b = phase(pair, hidden_a, hidden_b)

    out_y = [row_to(pair, "out_y", -ky) for ky in range(1, NY)]
    hid_a = gather_hidden(hidden_a, "hid_a")
    out_all = assemble([pair] + out_y)
    out_mine = out_all[:, 0].reshape(-1, feats)
    out_theirs = out_all[:, 1].reshape(-1, feats)
    out_mine, out_theirs, w_down_other = phase(out_mine, out_theirs, w_down_other)

    out_other = col_to(out_theirs, "out_core", dc=1)
    cut = NZ * tok
    far = hidden_units(out_mine[cut:], out_other[cut:], w_down, w_down_other, steps)
    far = [far[k * tok:(k + 1) * tok] for k in range(NZ)]
    far = [far[0]] + [p.astype(BF16) for p in far[1:]]
    *far, hid_a, out_mine, out_other = phase(*far, hid_a, out_mine, out_other)

    x_in = col_to(far[2], "rs_x", dx=1)
    b_in = col_to(far[1], "rs_b", dz=1)
    a_in = col_to(far[3], "rs_a", dz=-1)
    near = hidden_units(out_mine[:cut], out_other[:cut], w_down, w_down_other, steps)
    near = [near[k * tok:(k + 1) * tok] for k in range(NZ)]
    x_sum = (far[0] + b_in.astype(F32) + a_in.astype(F32)).astype(BF16)
    x_in, x_sum = phase(x_in, x_sum)
    pair = (near[2] + x_in.astype(F32)).astype(BF16)
    pair, x_sum, near0, near1, near3 = phase(pair, x_sum, near[0], near[1], near[3])
    b_half = col_to(pair[:half], "rs_fb", dz=1)
    a_half = col_to(pair[half:], "rs_fa", dz=-1)
    x_last = col_to(x_sum, "rs_xl", dx=1)
    b_sum = jnp.concatenate([near1[:half] + b_half.astype(F32), near1[half:]], axis=0).astype(BF16)
    a_sum = jnp.concatenate([near3[:half], near3[half:] + a_half.astype(F32)], axis=0).astype(BF16)
    b_sum, a_sum = phase(b_sum, a_sum)
    b_last = col_to(b_sum, "rs_bl", dz=1)
    a_last = col_to(a_sum, "rs_al", dz=-1)
    d_hidden = near0 + x_last.astype(F32) + b_last.astype(F32) + a_last.astype(F32)
    silu = gates * sig
    d_gate = (d_hidden * ups * sig * (1.0 + gates * (1.0 - sig))).astype(BF16)
    d_up = (d_hidden * silu).astype(BF16)
    both, own = phase(jnp.concatenate([d_gate, d_up], axis=0), inputs)

    both_x = col_to(both, "ag_x", dx=1)
    both_b = col_to(both, "ag_b", dz=1)
    both_a = col_to(both, "ag_a", dz=-1)
    copies = jnp.broadcast_to(own[None], (NY * NL, rows, feats))
    with jax.named_scope("input_rows"):
        whole = lax.all_to_all(copies, "row", 0, 0, tiled=True)
    both_x = phase(both_x, both_b, both_a)[0]
    both, both_x, both_b, both_a, hid_a = phase(both, both_x, both_b, both_a, hid_a)

    far_b = col_to(both_b[:tok], "ag_fb", dz=1)
    far_a = col_to(both_a[tok:], "ag_fa", dz=-1)
    swapped = swap([both], "ag_core")
    both_f = jnp.concatenate([far_b, far_a], axis=0)
    values_all = whole.astype(F32)
    squares = jnp.sum(values_all * values_all, axis=2)
    squares = squares + col_to(squares, "squares", dc=1)
    squares = squares + col_to(squares, "squares", dx=1)
    both, *swapped, both_f, both_x, both_a, both_b, whole, squares, hid_a = phase(
        both, *swapped, both_f, both_x, both_a, both_b, whole, squares, hid_a
    )

    both_xb = col_to(both_x, "ag_xb", dz=1)
    both_xa = col_to(both_x, "ag_xa", dz=-1)
    both_xf = col_to(both_f, "ag_xf", dx=1)
    swapped += swap([both_a, both_f, both_b, both_x], "ag_core")
    first = [both, both_a, both_f, both_b, *swapped[:4], both_x, swapped[4]]
    term_first = input_grads(first, w_gate, w_up, steps)
    hid_a_other = col_to(hid_a, "hid_core", dc=1)
    out_down = jnp.where(h == 0, out_all, out_all[::-1]).transpose(1, 2, 0, 3, 4)
    out_down = lax.dynamic_slice_in_dim(jnp.concatenate([out_down, out_down], axis=1), (NZ - z) % NZ, NZ, axis=1)
    out_down = out_down.reshape(-1, feats)
    down_a = down_grads(hid_a, hid_a_other, out_down, 1)
    pairs = []
    for at in range(NY):
        even, odd = whole[at * NL].reshape(NC, tok, feats), whole[at * NL + 1].reshape(NC, tok, feats)
        one = jnp.stack([jnp.where(h == 0, even, odd), jnp.where(h == 0, odd, even)])
        pairs.append(jnp.where(c == 0, one, one[:, ::-1])[:, :, None])
    in_all = jnp.zeros((NX, NC, NZ, tok, feats), BF16)
    for at, one in enumerate(pairs):
        in_all = lax.dynamic_update_slice(in_all, one, (0, 0, (at - z) % NZ, 0, 0))
    in_t = in_all.reshape(-1, feats).T
    squares = squares + neighbour(squares, "squares")
    both_xb, both_xa, both_xf, term_first, in_t, down_a, squares, hidden_b = phase(
        both_xb, both_xa, both_xf, term_first, in_t, down_a, squares, hidden_b
    )

    hid_b = gather_hidden(hidden_b, "hid_b")
    squares = squares + col_to(squares, "squares", dz=2)
    rstd_all = lax.rsqrt(squares / total_feats + EPS)
    rstd = lax.dynamic_index_in_dim(rstd_all, row, 0, keepdims=False)
    rstd_all = rstd_all.reshape(NY, NL, NC, tok)
    rstd_all = lax.dynamic_slice_in_dim(jnp.concatenate([rstd_all, rstd_all]), z, NZ).transpose(1, 2, 0, 3)
    rstd_all = jnp.where(h == 0, rstd_all, rstd_all[::-1])
    rstd_all = jnp.where(c == 0, rstd_all, rstd_all[:, ::-1]).reshape(1, -1)
    normed_t = (in_t.astype(F32) * rstd_all * gain[:, None]).astype(BF16)
    swapped_x = swap([both_xa, both_xf, both_xb], "ag_core")
    second = [both_xa, both_xf, both_xb, *swapped_x]
    term_second = input_grads(second, w_gate, w_up, steps)
    order_of = first[:8] + [first[8]] + second[:3] + [first[9]] + second[3:]
    term = jnp.concatenate([
        term_first[:9 * tok], term_second[:3 * tok], term_first[9 * tok:], term_second[3 * tok:]
    ], axis=0).reshape(NX, NC, NZ, tok, feats)

    def term_of(ky):
        return lax.dynamic_slice(term, (0, 0, (y + ky - z) % NZ, 0, 0), (NX, NC, 1, tok, feats))[:, :, 0]

    mine, normed_t, rstd, *sent = phase(
        term_of(0), normed_t, rstd, *[term_of(ky).astype(BF16) for ky in range(1, NY)]
    )
    received = [row_to(piece, "dn_y", ky + 1) for ky, piece in enumerate(sent)]
    grad_gate, grad_up = gate_up_grads(normed_t, order_of, steps)
    d_normed = mine
    for piece in received:
        d_normed = d_normed + piece.astype(F32)
    near, far = (jnp.where(same, d_normed[i], d_normed[1 - i]) for i in range(2))
    near, far, grad_gate, grad_up, hid_b = phase(near, far.astype(BF16), grad_gate, grad_up, hid_b)

    d_normed = near + row_to(far, "dn_xl", dl=1).astype(F32)
    d_normed = jnp.where(c == 0, d_normed, d_normed[::-1]).reshape(rows, feats)
    hid_b_other = col_to(hid_b, "hid_core", dc=1)
    values = inputs.astype(F32)
    proj = jnp.sum(d_normed * gain[None, :] * values, axis=1).reshape(1, rows)
    grad_gain = jnp.sum(d_normed * values * rstd[:, None], axis=0).reshape(1, feats)
    proj, grad_gain, hid_b_other = phase(proj, grad_gain, hid_b_other)

    proj = proj + col_to(proj, "proj", dc=1)
    grad_gain = grad_gain + row_to(grad_gain, "gain", dl=1)
    proj, grad_gain = phase(proj, grad_gain)
    proj = proj + col_to(proj, "proj", dx=1)
    grad_gain = grad_gain + neighbour_row(grad_gain, "gain")
    proj, grad_gain = phase(proj, grad_gain)
    proj = proj + neighbour(proj, "proj")
    grad_gain = grad_gain + row_to(grad_gain, "gain", dy=2)
    proj, grad_gain = phase(proj, grad_gain)
    down_b = down_grads(hid_b, hid_b_other, out_down, 1)
    grad_down = jnp.concatenate([down_a, down_b], axis=0)
    proj = (proj + col_to(proj, "proj", dz=2)).reshape(rows)
    scaled = rstd * rstd * rstd * proj / total_feats
    d_input = (
        out_grad.astype(F32) + rstd[:, None] * d_normed * gain[None, :] - values * scaled[:, None]
    ).astype(BF16)
    return (d_input, grad_gain.reshape(feats), grad_gate, grad_up, grad_down)


def solution(mesh):
    in_specs = (
        P("row", "col"),
        P("row", "col"),
        P("col"),
        P("col", "row"),
        P("col", "row"),
        P("row", "col"),
        P("col", "row"),
        P("col", "row"),
    )
    out_specs = (P("row", "col"), P("col"), P("col", "row"), P("col", "row"), P("row", "col"))
    return jax.shard_map(local, mesh=mesh, in_specs=in_specs, out_specs=out_specs, check_vma=False)
```

```python
import jax
import jax.numpy as jnp
from jax import lax
from jax.experimental import pallas as pl
from jax.experimental.pallas import tpu as pltpu
from jax.sharding import PartitionSpec as P

EPS = 1e-05
NZ, NX, NC = 4, 2, 2
NY, NL = 4, 2
F32, BF16 = jnp.float32, jnp.bfloat16


def dot(left, right, a, b):
    return lax.dot_general(left, right, (((a,), (b,)), ((), ())), preferred_element_type=F32)


def kernel_call(body, name, steps, in_specs, out_specs, out_shape, scratch, args):
    return pl.pallas_call(
        body,
        grid=(steps,),
        in_specs=in_specs,
        out_specs=out_specs,
        out_shape=out_shape,
        scratch_shapes=scratch,
        compiler_params=pltpu.CompilerParams(vmem_limit_bytes=60 * 2**20),
        name=name,
    )(*args)


def hidden_units(left, left_other, w, w_other, part, kinds, steps):
    f, (width, m) = left.shape[1], (w.shape[0], left.shape[0] // NX)
    n, tok = width // steps, m // len(kinds)

    def body(l, lo, w, wo, *outs):
        total = dot(l[...], w[...], 1, 1) + dot(lo[...], wo[...], 1, 1)
        for at, out in enumerate(outs):
            out[...] = total[at * tok:(at + 1) * tok].astype(out.dtype)

    lefts = [pl.BlockSpec((m, f), lambda i: (part, 0))] * 2
    rights = [pl.BlockSpec((n, f), lambda i: (i, 0))] * 2
    return kernel_call(
        body, "hidden_units", steps, lefts + rights, [pl.BlockSpec((tok, n), lambda i: (0, i))] * len(kinds),
        [jax.ShapeDtypeStruct((tok, width), kind) for kind in kinds], [], (left, left_other, w, w_other),
    )


def at_block(rows, n, block):
    return pl.BlockSpec((rows, n), lambda i: (block, i))


def input_grads(gate, up, w_gate, w_up, tok, steps):
    f, width = w_gate.shape
    k, count = width // steps, len(gate)

    def body(*refs):
        gates, ups, (wg, wu, out) = refs[:count], refs[count:2 * count], refs[2 * count:]
        total = dot(jnp.concatenate([p[...] for p in gates], axis=0), wg[...], 1, 1)
        total += dot(jnp.concatenate([p[...] for p in ups], axis=0), wu[...], 1, 1)

        @pl.when(pl.program_id(0) == 0)
        def _():
            out[...] = total

        @pl.when(pl.program_id(0) > 0)
        def _():
            out[...] += total

    specs = [at_block(tok, k, block) for _, block in gate + up] + [at_block(f, k, 0)] * 2
    m = tok * count
    return kernel_call(
        body, "input_grads", steps, specs, pl.BlockSpec((m, f), lambda i: (0, 0)),
        jax.ShapeDtypeStruct((m, f), F32), [], (*[x for x, _ in gate + up], w_gate, w_up),
    )


def gate_up_grads(normed_t, gate, up, tok, steps):
    f, t = normed_t.shape
    width, count = gate[0][0].shape[1], len(gate)
    n = width // steps

    def body(left, *refs):
        gates, ups, (gate_out, up_out) = refs[:count], refs[count:2 * count], refs[2 * count:]
        left = left[...]
        gate_out[...] = dot(left, jnp.concatenate([p[...] for p in gates], axis=0), 1, 0).astype(BF16)
        up_out[...] = dot(left, jnp.concatenate([p[...] for p in ups], axis=0), 1, 0).astype(BF16)

    specs = [pl.BlockSpec((f, t), lambda i: (0, 0))] + [at_block(tok, n, block) for _, block in gate + up]
    return kernel_call(
        body, "gate_up_grads", steps, specs, [at_block(f, n, 0)] * 2,
        [jax.ShapeDtypeStruct((f, width), BF16)] * 2, [], (normed_t, *[x for x, _ in gate + up]),
    )


def down_grads(hid, hid_other, out, width, first, earlier, steps):
    f, (t, some) = out.shape[1], hid.shape
    n = some // steps

    def body(left, left_other, right, *refs):
        refs[-1][...] = (dot(left[...], right[:t], 0, 0) + dot(left_other[...], right[t:], 0, 0)).astype(BF16)

    specs = [at_block(t, n, 0)] * 2 + [pl.BlockSpec((2 * t, f), lambda i: (0, 0))]
    more = () if earlier is None else (earlier,)
    return pl.pallas_call(
        body,
        grid=(steps,),
        in_specs=specs + [pl.BlockSpec(memory_space=pl.ANY)] * len(more),
        out_specs=pl.BlockSpec((n, f), lambda i: (first + i, 0)),
        out_shape=jax.ShapeDtypeStruct((width, f), BF16),
        input_output_aliases={3: 0} if more else {},
        compiler_params=pltpu.CompilerParams(vmem_limit_bytes=60 * 2**20),
        name="down_grads",
    )(hid, hid_other, out, *more)


def col_to(x, name, dz=0, dx=0, dc=0):
    pairs = []
    for z in range(NZ):
        for h in range(NX):
            for c in range(NC):
                dst = (((z + dz) % NZ) * NX + (h + dx) % NX) * NC + (c + dc) % NC
                pairs.append(((z * NX + h) * NC + c, dst))
    with jax.named_scope(name):
        return lax.ppermute(x, "col", pairs)


def row_to(x, name, dy=0, dl=0):
    pairs = []
    for y in range(NY):
        for l in range(NL):
            pairs.append((y * NL + l, ((y + dy) % NY) * NL + (l + dl) % NL))
    with jax.named_scope(name):
        return lax.ppermute(x, "row", pairs)


def phase(*arrays):
    return lax.optimization_barrier(arrays)


def local(inputs, out_grad, gain, w_gate, w_up, w_down, gate_pre, up_pre):
    rows, feats = inputs.shape
    width = gate_pre.shape[1]
    tok = gate_pre.shape[0]
    half = tok // 2
    total_feats = feats * NZ * NX * NC
    steps = 2 if width % 256 == 0 else 1
    ahead = width // 4
    col, row = lax.axis_index("col"), lax.axis_index("row")
    z, h, c = col // (NX * NC), (col // NC) % NX, col % NC
    y, l = row // NL, row % NL

    same = (l + h) % NX == 0

    def order(mine, other):
        f = mine.shape[1]
        mine, other = mine.reshape(NC, tok, f), other.reshape(NC, tok, f)
        pair = jnp.stack([jnp.where(same, mine, other), jnp.where(same, other, mine)])
        return jnp.where(c == 0, pair, pair[:, ::-1])[:, :, None]

    def assemble(pairs):
        both = [jnp.zeros((NX, NZ, *pairs[0].shape[3:]), pairs[0].dtype) for _ in range(NC)]
        for ky, pair in enumerate(pairs):
            at = (0, (y + ky - z) % NZ, 0, 0)
            both = [lax.dynamic_update_slice(full, pair[:, i], at) for i, full in enumerate(both)]
        return [full.reshape(-1, full.shape[3]) for full in both]

    def neighbour(x, name):
        with jax.named_scope(name):
            return lax.ppermute(x, "col", [(i, i ^ NC * NX) for i in range(NZ * NX * NC)])

    def neighbour_row(x, name):
        with jax.named_scope(name):
            return lax.ppermute(x, "row", [(i, i ^ NL) for i in range(NY * NL)])

    def gather_hidden(x, name):
        groups = [[chip * NC + core for chip in range(NZ * NX)] for core in range(NC)]
        copies = jnp.broadcast_to(x[None], (NZ * NX, *x.shape))
        with jax.named_scope(name):
            return lax.all_to_all(copies, "col", 0, 0, axis_index_groups=groups, tiled=True).reshape(-1, x.shape[1])

    out_xl = row_to(out_grad, "out_xl", dl=1)
    w_down_other = col_to(w_down, "w_down", dc=1)
    gates = gate_pre.astype(F32)
    ups = up_pre.astype(F32)
    sig = jax.nn.sigmoid(gates)
    hidden = (gates * sig * ups).astype(BF16)
    hidden_a, hidden_b = hidden[:, :ahead], hidden[:, ahead:]
    values = inputs.astype(F32)
    squares = jnp.sum(values * values, axis=1).reshape(1, rows)
    squares = squares + col_to(squares, "squares", dc=1)
    pair = order(out_grad, out_xl)
    pair, hidden_a, hidden_b, w_down_other, squares = phase(pair, hidden_a, hidden_b, w_down_other, squares)

    out_y = [row_to(pair, "out_y", -ky) for ky in range(1, NY)]
    hid_a = gather_hidden(hidden_a, "hid_a")
    squares = squares + neighbour(squares, "squares")
    out_mine, out_theirs = assemble([pair] + out_y)
    out_mine, out_theirs, squares = phase(out_mine, out_theirs, squares)

    out_other = col_to(out_theirs, "out_core", dc=1)
    far0, far1, far2, far3 = hidden_units(
        out_mine, out_other, w_down, w_down_other, 1, (F32, BF16, BF16, BF16), steps
    )
    far0, far1, far2, far3, out_mine, out_other, hid_a, squares = phase(
        far0, far1, far2, far3, out_mine, out_other, hid_a, squares
    )

    x_in = col_to(far2, "rs_x", dx=1)
    b_in = col_to(far1, "rs_b", dz=1)
    a_in = col_to(far3, "rs_a", dz=-1)
    near0, near1, near2, near3 = hidden_units(out_mine, out_other, w_down, w_down_other, 0, (F32,) * NZ, steps)
    squares = phase(squares, near0)[0]
    squares = squares + col_to(squares, "squares", dz=2)
    x_in, b_in, a_in, near0, near1, near2, near3, squares, hid_a = phase(
        x_in, b_in, a_in, near0, near1, near2, near3, squares, hid_a
    )
    b_half = col_to((near2[:half] + x_in[:half].astype(F32)).astype(BF16), "rs_fb", dz=1)
    a_half = col_to((near2[half:] + x_in[half:].astype(F32)).astype(BF16), "rs_fa", dz=-1)
    x_last = col_to((far0 + b_in.astype(F32) + a_in.astype(F32)).astype(BF16), "rs_xl", dx=1)
    b_sum = jnp.concatenate([near1[:half] + b_half.astype(F32), near1[half:]], axis=0).astype(BF16)
    a_sum = jnp.concatenate([near3[:half], near3[half:] + a_half.astype(F32)], axis=0).astype(BF16)
    b_sum, a_sum, out_mine, out_theirs, squares, hid_a = phase(b_sum, a_sum, out_mine, out_theirs, squares, hid_a)
    b_last = col_to(b_sum, "rs_bl", dz=1)
    a_last = col_to(a_sum, "rs_al", dz=-1)
    squares = squares + col_to(squares, "squares", dx=1)
    rstd = lax.rsqrt(squares.reshape(rows) / total_feats + EPS)
    normed = (values * rstd[:, None] * gain[None, :]).astype(BF16)
    copies = jnp.broadcast_to(normed[None], (NY * NL, rows, feats))
    with jax.named_scope("normed_rows"):
        whole = lax.all_to_all(copies, "row", 0, 0, tiled=True)
    d_hidden = near0 + x_last.astype(F32) + b_last.astype(F32) + a_last.astype(F32)
    silu = gates * sig
    d_gate = (d_hidden * ups * sig * (1.0 + gates * (1.0 - sig))).astype(BF16)
    d_up = (d_hidden * silu).astype(BF16)
    both = jnp.concatenate([d_gate, d_up], axis=0)
    d_gate, d_up, both, hid_a, rstd, out_mine, out_theirs = phase(
        d_gate, d_up, both, hid_a, rstd, out_mine, out_theirs
    )

    gate_b = col_to(d_gate, "ag_gate_b", dz=1)
    up_a = col_to(d_up, "ag_up_a", dz=-1)
    up_b = col_to(d_up, "ag_up_b", dz=1)
    gate_a = col_to(d_gate, "ag_gate_a", dz=-1)
    both_x = col_to(both, "ag_x", dx=1)
    def by_chip(x):
        x = x.reshape(NX, NZ, tok, feats)
        x = jnp.where(h == 0, x, x[::-1]).transpose(1, 0, 2, 3)
        return lax.dynamic_slice_in_dim(jnp.concatenate([x, x]), (NZ - z) % NZ, NZ).reshape(-1, feats)

    out_down = jnp.concatenate([by_chip(out_mine), by_chip(out_theirs)], axis=0)
    pairs = []
    for at in range(NY):
        even, odd = whole[at * NL].reshape(NC, tok, feats), whole[at * NL + 1].reshape(NC, tok, feats)
        one = jnp.stack([jnp.where(h == 0, even, odd), jnp.where(h == 0, odd, even)])
        pairs.append(jnp.where(c == 0, one, one[:, ::-1])[:, :, None])
    normed_all = jnp.zeros((NX, NC, NZ, tok, feats), BF16)
    for at, one in enumerate(pairs):
        normed_all = lax.dynamic_update_slice(normed_all, one, (0, 0, (at - z) % NZ, 0, 0))
    normed_t = normed_all.reshape(-1, feats).T
    gate_b, up_a, up_b, gate_a, both_x, both, hid_a, normed_t, out_down = phase(
        gate_b, up_a, up_b, gate_a, both_x, both, hid_a, normed_t, out_down
    )

    gate_f = col_to(gate_b, "ag_gate_f", dz=1)
    up_f = col_to(up_a, "ag_up_f", dz=-1)
    hid_a_other = col_to(hid_a, "hid_core", dc=1)
    swap_late = phase(both, up_a, gate_a, gate_b, up_b, both_x, hid_a_other)
    swapped = [col_to(piece, "ag_core", dc=1) for piece in swap_late[:6]]
    gate_f, up_f, both, gate_b, up_a, up_b, gate_a, both_x, normed_t, hid_a, hid_a_other, *swapped = phase(
        gate_f, up_f, both, gate_b, up_a, up_b, gate_a, both_x, normed_t, hid_a, hid_a_other, *swapped
    )

    both_xb = col_to(both_x, "ag_xb", dz=1)
    both_xa = col_to(both_x, "ag_xa", dz=-1)
    gate_xf = col_to(gate_f, "ag_gate_xf", dx=1)
    up_xf = col_to(up_f, "ag_up_xf", dx=1)
    swapped_f = [col_to(piece, "ag_core", dc=1) for piece in (gate_f, up_f)]

    near_ones = [both, up_a, gate_a, gate_f, up_f, gate_b, up_b, both_x]
    swapped = swapped[:3] + swapped_f + swapped[3:]

    def by_k(both, up_a, gate_a, gate_f, up_f, gate_b, up_b, both_x):
        gate = [(both, 0), (gate_a, 0), (gate_f, 0), (gate_b, 0)]
        up = [(both, 1), (up_a, 0), (up_f, 0), (up_b, 0)]
        return gate, up, [(both_x, 0)], [(both_x, 1)]

    gate_mine, up_mine, gate_x, up_x = by_k(*near_ones)
    gate_theirs, up_theirs, gate_xt, up_xt = by_k(*swapped)
    gate_first = gate_mine + gate_theirs + gate_x + gate_xt
    up_first = up_mine + up_theirs + up_x + up_xt
    term_first = input_grads(gate_first, up_first, w_gate, w_up, tok, steps)

    term_first, hid_a = phase(term_first, hid_a)
    down_a = down_grads(hid_a, hid_a_other, out_down, width, 0, None, 1)
    both_xb, both_xa, gate_xf, up_xf, term_first, hidden_b, down_a = phase(
        both_xb, both_xa, gate_xf, up_xf, term_first, hidden_b, down_a
    )
    hid_b = gather_hidden(hidden_b, "hid_b")

    far_ones = [both_xa, gate_xf, up_xf, both_xb]
    swapped_far = [col_to(piece, "ag_core", dc=1) for piece in far_ones]

    def by_k_far(both_xa, gate_xf, up_xf, both_xb):
        return [(both_xa, 0), (gate_xf, 0), (both_xb, 0)], [(both_xa, 1), (up_xf, 0), (both_xb, 1)]

    gate_xmine, up_xmine = by_k_far(*far_ones)
    gate_xtheirs, up_xtheirs = by_k_far(*swapped_far)
    term_second = input_grads(gate_xmine + gate_xtheirs, up_xmine + up_xtheirs, w_gate, w_up, tok, steps)
    gate_all = gate_mine + gate_theirs + gate_x + gate_xmine + gate_xt + gate_xtheirs
    up_all = up_mine + up_theirs + up_x + up_xmine + up_xt + up_xtheirs
    term = jnp.concatenate([
        term_first[:9 * tok], term_second[:3 * tok], term_first[9 * tok:], term_second[3 * tok:]
    ], axis=0).reshape(NX, NC, NZ, tok, feats)
    def term_of(ky):
        return lax.dynamic_slice(term, (0, 0, (y + ky - z) % NZ, 0, 0), (NX, NC, 1, tok, feats))[:, :, 0]

    mine, normed_t, *sent = phase(term_of(0), normed_t, *[term_of(ky).astype(BF16) for ky in range(1, NY)])
    received = [row_to(piece, "dn_y", ky + 1) for ky, piece in enumerate(sent)]
    grad_gate, grad_up = gate_up_grads(normed_t, gate_all, up_all, tok, steps)
    d_normed = mine
    for piece in received:
        d_normed = d_normed + piece.astype(F32)
    near, far = (jnp.where(same, d_normed[i], d_normed[1 - i]) for i in range(2))
    near, far, grad_gate, grad_up = phase(near, far.astype(BF16), grad_gate, grad_up)

    d_normed = near + row_to(far, "dn_xl", dl=1).astype(F32)
    d_normed = jnp.where(c == 0, d_normed, d_normed[::-1]).reshape(rows, feats)
    proj = jnp.sum(d_normed * gain[None, :] * values, axis=1).reshape(1, rows)
    grad_gain = jnp.sum(d_normed * values * rstd[:, None], axis=0).reshape(1, feats)
    proj, grad_gain = phase(proj, grad_gain)

    proj = proj + col_to(proj, "proj", dc=1)
    proj, grad_gain = phase(proj, grad_gain)
    proj = proj + col_to(proj, "proj", dx=1)
    grad_gain = grad_gain + row_to(grad_gain, "gain", dl=1)
    proj, grad_gain, hid_b = phase(proj, grad_gain, hid_b)
    hid_b_other = col_to(hid_b, "hid_core", dc=1)
    proj = proj + neighbour(proj, "proj")
    grad_gain = grad_gain + neighbour_row(grad_gain, "gain")
    proj, grad_gain, hid_b, hid_b_other = phase(proj, grad_gain, hid_b, hid_b_other)
    grad_gain = grad_gain + row_to(grad_gain, "gain", dy=2)
    grad_down = down_grads(hid_b, hid_b_other, out_down, width, 1, down_a, 3)
    proj = (proj + col_to(proj, "proj", dz=2)).reshape(rows)
    scaled = rstd * rstd * rstd * proj / total_feats
    d_input = (
        out_grad.astype(F32) + rstd[:, None] * d_normed * gain[None, :] - values * scaled[:, None]
    ).astype(BF16)
    return (d_input, grad_gain.reshape(feats), grad_gate, grad_up, grad_down)


def solution(mesh):
    in_specs = (
        P("row", "col"),
        P("row", "col"),
        P("col"),
        P("col", "row"),
        P("col", "row"),
        P("row", "col"),
        P("col", "row"),
        P("col", "row"),
    )
    out_specs = (P("row", "col"), P("col"), P("col", "row"), P("col", "row"), P("row", "col"))
    return jax.shard_map(local, mesh=mesh, in_specs=in_specs, out_specs=out_specs, check_vma=False)
```

```python
import jax
import jax.numpy as jnp
from jax import lax
from jax.experimental import pallas as pl
from jax.experimental.pallas import tpu as pltpu
from jax.sharding import PartitionSpec as P

EPS = 1e-05
NZ, NX, NC = 4, 2, 2
NY, NL = 4, 2
F32, BF16 = jnp.float32, jnp.bfloat16


def dot(left, right, a, b):
    return lax.dot_general(left, right, (((a,), (b,)), ((), ())), preferred_element_type=F32)


def kernel_call(body, name, steps, in_specs, out_specs, out_shape, scratch, args):
    return pl.pallas_call(
        body,
        grid=(steps,),
        in_specs=in_specs,
        out_specs=out_specs,
        out_shape=out_shape,
        scratch_shapes=scratch,
        compiler_params=pltpu.CompilerParams(vmem_limit_bytes=60 * 2**20),
        name=name,
    )(*args)


def hidden_units(left, left_other, w, w_other, part, kinds, steps):
    f, (width, m) = left.shape[1], (w.shape[0], left.shape[0] // NX)
    n, tok = width // steps, m // len(kinds)

    def body(l, lo, w, wo, *outs):
        total = dot(l[...], w[...], 1, 1) + dot(lo[...], wo[...], 1, 1)
        for at, out in enumerate(outs):
            out[...] = total[at * tok:(at + 1) * tok].astype(out.dtype)

    lefts = [pl.BlockSpec((m, f), lambda i: (part, 0))] * 2
    rights = [pl.BlockSpec((n, f), lambda i: (i, 0))] * 2
    return kernel_call(
        body, "hidden_units", steps, lefts + rights, [pl.BlockSpec((tok, n), lambda i: (0, i))] * len(kinds),
        [jax.ShapeDtypeStruct((tok, width), kind) for kind in kinds], [], (left, left_other, w, w_other),
    )


def at_block(rows, n, block):
    return pl.BlockSpec((rows, n), lambda i: (block, i))


def input_grads(gate, up, w_gate, w_up, tok, steps):
    f, width = w_gate.shape
    k, count = width // steps, len(gate)

    def body(*refs):
        gates, ups, (wg, wu, out) = refs[:count], refs[count:2 * count], refs[2 * count:]
        total = dot(jnp.concatenate([p[...] for p in gates], axis=0), wg[...], 1, 1)
        total += dot(jnp.concatenate([p[...] for p in ups], axis=0), wu[...], 1, 1)

        @pl.when(pl.program_id(0) == 0)
        def _():
            out[...] = total

        @pl.when(pl.program_id(0) > 0)
        def _():
            out[...] += total

    specs = [at_block(tok, k, block) for _, block in gate + up] + [at_block(f, k, 0)] * 2
    m = tok * count
    return kernel_call(
        body, "input_grads", steps, specs, pl.BlockSpec((m, f), lambda i: (0, 0)),
        jax.ShapeDtypeStruct((m, f), F32), [], (*[x for x, _ in gate + up], w_gate, w_up),
    )


def gate_up_grads(normed_t, gate, up, tok, steps):
    f, t = normed_t.shape
    width, count = gate[0][0].shape[1], len(gate)
    n = width // steps

    def body(left, *refs):
        gates, ups, (gate_out, up_out) = refs[:count], refs[count:2 * count], refs[2 * count:]
        left = left[...]
        gate_out[...] = dot(left, jnp.concatenate([p[...] for p in gates], axis=0), 1, 0).astype(BF16)
        up_out[...] = dot(left, jnp.concatenate([p[...] for p in ups], axis=0), 1, 0).astype(BF16)

    specs = [pl.BlockSpec((f, t), lambda i: (0, 0))] + [at_block(tok, n, block) for _, block in gate + up]
    return kernel_call(
        body, "gate_up_grads", steps, specs, [at_block(f, n, 0)] * 2,
        [jax.ShapeDtypeStruct((f, width), BF16)] * 2, [], (normed_t, *[x for x, _ in gate + up]),
    )


def down_grads(hid, hid_other, out, width, first, earlier, steps):
    f, (t, some) = out.shape[1], hid.shape
    n = some // steps

    def body(left, left_other, right, *refs):
        refs[-1][...] = (dot(left[...], right[:t], 0, 0) + dot(left_other[...], right[t:], 0, 0)).astype(BF16)

    specs = [at_block(t, n, 0)] * 2 + [pl.BlockSpec((2 * t, f), lambda i: (0, 0))]
    more = () if earlier is None else (earlier,)
    return pl.pallas_call(
        body,
        grid=(steps,),
        in_specs=specs + [pl.BlockSpec(memory_space=pl.ANY)] * len(more),
        out_specs=pl.BlockSpec((n, f), lambda i: (first + i, 0)),
        out_shape=jax.ShapeDtypeStruct((width, f), BF16),
        input_output_aliases={3: 0} if more else {},
        compiler_params=pltpu.CompilerParams(vmem_limit_bytes=60 * 2**20),
        name="down_grads",
    )(hid, hid_other, out, *more)


def col_to(x, name, dz=0, dx=0, dc=0):
    pairs = []
    for z in range(NZ):
        for h in range(NX):
            for c in range(NC):
                dst = (((z + dz) % NZ) * NX + (h + dx) % NX) * NC + (c + dc) % NC
                pairs.append(((z * NX + h) * NC + c, dst))
    with jax.named_scope(name):
        return lax.ppermute(x, "col", pairs)


def row_to(x, name, dy=0, dl=0):
    pairs = []
    for y in range(NY):
        for l in range(NL):
            pairs.append((y * NL + l, ((y + dy) % NY) * NL + (l + dl) % NL))
    with jax.named_scope(name):
        return lax.ppermute(x, "row", pairs)


def phase(*arrays):
    return lax.optimization_barrier(arrays)


def local(inputs, out_grad, gain, w_gate, w_up, w_down, gate_pre, up_pre):
    rows, feats = inputs.shape
    width = gate_pre.shape[1]
    tok = gate_pre.shape[0]
    half = tok // 2
    total_feats = feats * NZ * NX * NC
    steps = 2 if width % 256 == 0 else 1
    ahead = width // 4
    col, row = lax.axis_index("col"), lax.axis_index("row")
    z, h, c = col // (NX * NC), (col // NC) % NX, col % NC
    y, l = row // NL, row % NL

    same = (l + h) % NX == 0

    def order(mine, other):
        f = mine.shape[1]
        mine, other = mine.reshape(NC, tok, f), other.reshape(NC, tok, f)
        pair = jnp.stack([jnp.where(same, mine, other), jnp.where(same, other, mine)])
        return jnp.where(c == 0, pair, pair[:, ::-1])[:, :, None]

    def assemble(pairs):
        both = [jnp.zeros((NX, NZ, *pairs[0].shape[3:]), pairs[0].dtype) for _ in range(NC)]
        for ky, pair in enumerate(pairs):
            at = (0, (y + ky - z) % NZ, 0, 0)
            both = [lax.dynamic_update_slice(full, pair[:, i], at) for i, full in enumerate(both)]
        return [full.reshape(-1, full.shape[3]) for full in both]

    def neighbour(x, name):
        with jax.named_scope(name):
            return lax.ppermute(x, "col", [(i, i ^ NC * NX) for i in range(NZ * NX * NC)])

    def neighbour_row(x, name):
        with jax.named_scope(name):
            return lax.ppermute(x, "row", [(i, i ^ NL) for i in range(NY * NL)])

    def gather_hidden(x, name):
        groups = [[chip * NC + core for chip in range(NZ * NX)] for core in range(NC)]
        copies = x if x.ndim == 3 else jnp.broadcast_to(x[None], (NZ * NX, *x.shape))
        with jax.named_scope(name):
            return lax.all_to_all(copies, "col", 0, 0, axis_index_groups=groups, tiled=True).reshape(-1, x.shape[-1])

    out_xl = row_to(out_grad, "out_xl", dl=1)
    w_down_other = col_to(w_down, "w_down", dc=1)
    gates = gate_pre.astype(F32)
    ups = up_pre.astype(F32)
    sig = jax.nn.sigmoid(gates)
    hidden = (gates * sig * ups).astype(BF16)
    hidden_a, hidden_b = hidden[:, :ahead], hidden[:, ahead:]
    values = inputs.astype(F32)
    squares = jnp.sum(values * values, axis=1).reshape(1, rows)
    squares = squares + col_to(squares, "squares", dc=1)
    pair = order(out_grad, out_xl)
    pair, hidden_a, hidden_b, w_down_other, squares = phase(pair, hidden_a, hidden_b, w_down_other, squares)

    out_y = [row_to(pair, "out_y", -ky) for ky in range(1, NY)]
    hid_a = gather_hidden(hidden_a, "hid_a")
    squares = squares + neighbour(squares, "squares")
    out_mine, out_theirs = assemble([pair] + out_y)
    hid_copies = jnp.broadcast_to(hidden_b[None], (NZ * NX, *hidden_b.shape))
    out_mine, out_theirs, squares, hid_copies = phase(out_mine, out_theirs, squares, hid_copies)

    out_other = col_to(out_theirs, "out_core", dc=1)
    far0, far1, far2, far3 = hidden_units(
        out_mine, out_other, w_down, w_down_other, 1, (F32, BF16, BF16, BF16), steps
    )
    far0, far1, far2, far3, out_mine, out_other, hid_a, squares = phase(
        far0, far1, far2, far3, out_mine, out_other, hid_a, squares
    )

    x_in = col_to(far2, "rs_x", dx=1)
    b_in = col_to(far1, "rs_b", dz=1)
    a_in = col_to(far3, "rs_a", dz=-1)
    near0, near1, near2, near3 = hidden_units(out_mine, out_other, w_down, w_down_other, 0, (F32,) * NZ, steps)
    squares = phase(squares, near0)[0]
    squares = squares + col_to(squares, "squares", dz=2)
    x_in, b_in, a_in, near0, near1, near2, near3, squares, hid_a = phase(
        x_in, b_in, a_in, near0, near1, near2, near3, squares, hid_a
    )
    b_half = col_to((near2[:half] + x_in[:half].astype(F32)).astype(BF16), "rs_fb", dz=1)
    a_half = col_to((near2[half:] + x_in[half:].astype(F32)).astype(BF16), "rs_fa", dz=-1)
    x_last = col_to((far0 + b_in.astype(F32) + a_in.astype(F32)).astype(BF16), "rs_xl", dx=1)
    b_sum = jnp.concatenate([near1[:half] + b_half.astype(F32), near1[half:]], axis=0).astype(BF16)
    a_sum = jnp.concatenate([near3[:half], near3[half:] + a_half.astype(F32)], axis=0).astype(BF16)
    b_sum, a_sum, out_mine, out_theirs, squares, hid_a = phase(b_sum, a_sum, out_mine, out_theirs, squares, hid_a)
    b_last = col_to(b_sum, "rs_bl", dz=1)
    a_last = col_to(a_sum, "rs_al", dz=-1)
    squares = squares + col_to(squares, "squares", dx=1)
    rstd = lax.rsqrt(squares.reshape(rows) / total_feats + EPS)
    normed = (values * rstd[:, None] * gain[None, :]).astype(BF16)
    copies = jnp.broadcast_to(normed[None], (NY * NL, rows, feats))
    with jax.named_scope("normed_rows"):
        whole = lax.all_to_all(copies, "row", 0, 0, tiled=True)
    d_hidden = near0 + x_last.astype(F32) + b_last.astype(F32) + a_last.astype(F32)
    silu = gates * sig
    d_gate = (d_hidden * ups * sig * (1.0 + gates * (1.0 - sig))).astype(BF16)
    d_up = (d_hidden * silu).astype(BF16)
    both = jnp.concatenate([d_gate, d_up], axis=0)
    d_gate, d_up, both, hid_a, rstd, out_mine, out_theirs = phase(
        d_gate, d_up, both, hid_a, rstd, out_mine, out_theirs
    )

    gate_b = col_to(d_gate, "ag_gate_b", dz=1)
    up_a = col_to(d_up, "ag_up_a", dz=-1)
    up_b = col_to(d_up, "ag_up_b", dz=1)
    gate_a = col_to(d_gate, "ag_gate_a", dz=-1)
    both_x = col_to(both, "ag_x", dx=1)
    def by_chip(x):
        x = x.reshape(NX, NZ, tok, feats)
        x = jnp.where(h == 0, x, x[::-1]).transpose(1, 0, 2, 3)
        return lax.dynamic_slice_in_dim(jnp.concatenate([x, x]), (NZ - z) % NZ, NZ).reshape(-1, feats)

    out_down = jnp.concatenate([by_chip(out_mine), by_chip(out_theirs)], axis=0)
    pairs = []
    for at in range(NY):
        even, odd = whole[at * NL].reshape(NC, tok, feats), whole[at * NL + 1].reshape(NC, tok, feats)
        one = jnp.stack([jnp.where(h == 0, even, odd), jnp.where(h == 0, odd, even)])
        pairs.append(jnp.where(c == 0, one, one[:, ::-1])[:, :, None])
    normed_all = jnp.zeros((NX, NC, NZ, tok, feats), BF16)
    for at, one in enumerate(pairs):
        normed_all = lax.dynamic_update_slice(normed_all, one, (0, 0, (at - z) % NZ, 0, 0))
    normed_t = normed_all.reshape(-1, feats).T
    swapped = [col_to(piece, "ag_core", dc=1) for piece in (up_a, gate_a, gate_b, up_b)]
    gate_b, up_a, up_b, gate_a, both_x, both, hid_a, normed_t, out_down, *swapped = phase(
        gate_b, up_a, up_b, gate_a, both_x, both, hid_a, normed_t, out_down, *swapped
    )

    gate_f = col_to(gate_b, "ag_gate_f", dz=1)
    up_f = col_to(up_a, "ag_up_f", dz=-1)
    hid_a_other = col_to(hid_a, "hid_core", dc=1)
    swapped = [col_to(both, "ag_core", dc=1), *swapped, col_to(both_x, "ag_core", dc=1)]
    gate_f, up_f, both, gate_b, up_a, up_b, gate_a, both_x, normed_t, hid_a, hid_a_other, *swapped = phase(
        gate_f, up_f, both, gate_b, up_a, up_b, gate_a, both_x, normed_t, hid_a, hid_a_other, *swapped
    )

    both_xb = col_to(both_x, "ag_xb", dz=1)
    both_xa = col_to(both_x, "ag_xa", dz=-1)
    gate_xf = col_to(gate_f, "ag_gate_xf", dx=1)
    up_xf = col_to(up_f, "ag_up_xf", dx=1)
    swapped_f = [col_to(piece, "ag_core", dc=1) for piece in (gate_f, up_f)]

    near_ones = [both, up_a, gate_a, gate_f, up_f, gate_b, up_b, both_x]
    swapped = swapped[:3] + swapped_f + swapped[3:]

    def by_k(both, up_a, gate_a, gate_f, up_f, gate_b, up_b, both_x):
        gate = [(both, 0), (gate_a, 0), (gate_f, 0), (gate_b, 0)]
        up = [(both, 1), (up_a, 0), (up_f, 0), (up_b, 0)]
        return gate, up, [(both_x, 0)], [(both_x, 1)]

    gate_mine, up_mine, gate_x, up_x = by_k(*near_ones)
    gate_theirs, up_theirs, gate_xt, up_xt = by_k(*swapped)
    gate_first = gate_mine + gate_theirs + gate_x + gate_xt
    up_first = up_mine + up_theirs + up_x + up_xt
    term_first = input_grads(gate_first, up_first, w_gate, w_up, tok, steps)

    term_first, hid_a = phase(term_first, hid_a)
    down_a = down_grads(hid_a, hid_a_other, out_down, width, 0, None, 1)
    both_xb, both_xa, gate_xf, up_xf, term_first, hid_copies, down_a = phase(
        both_xb, both_xa, gate_xf, up_xf, term_first, hid_copies, down_a
    )
    hid_b = gather_hidden(hid_copies, "hid_b")

    far_ones = [both_xa, gate_xf, up_xf, both_xb]
    swapped_far = [col_to(piece, "ag_core", dc=1) for piece in far_ones]

    def by_k_far(both_xa, gate_xf, up_xf, both_xb):
        return [(both_xa, 0), (gate_xf, 0), (both_xb, 0)], [(both_xa, 1), (up_xf, 0), (both_xb, 1)]

    gate_xmine, up_xmine = by_k_far(*far_ones)
    gate_xtheirs, up_xtheirs = by_k_far(*swapped_far)
    term_second = input_grads(gate_xmine + gate_xtheirs, up_xmine + up_xtheirs, w_gate, w_up, tok, steps)
    gate_all = gate_mine + gate_theirs + gate_x + gate_xmine + gate_xt + gate_xtheirs
    up_all = up_mine + up_theirs + up_x + up_xmine + up_xt + up_xtheirs
    term = jnp.concatenate([
        term_first[:9 * tok], term_second[:3 * tok], term_first[9 * tok:], term_second[3 * tok:]
    ], axis=0).reshape(NX, NC, NZ, tok, feats)
    def term_of(ky):
        return lax.dynamic_slice(term, (0, 0, (y + ky - z) % NZ, 0, 0), (NX, NC, 1, tok, feats))[:, :, 0]

    mine, normed_t, *sent = phase(term_of(0), normed_t, *[term_of(ky).astype(BF16) for ky in range(1, NY)])
    received = [row_to(piece, "dn_y", ky + 1) for ky, piece in enumerate(sent)]
    grad_gate, grad_up = gate_up_grads(normed_t, gate_all, up_all, tok, steps)
    d_normed = mine
    for piece in received:
        d_normed = d_normed + piece.astype(F32)
    near, far = (jnp.where(same, d_normed[i], d_normed[1 - i]) for i in range(2))
    near, far, grad_gate, grad_up = phase(near, far.astype(BF16), grad_gate, grad_up)

    d_normed = near + row_to(far, "dn_xl", dl=1).astype(F32)
    d_normed = jnp.where(c == 0, d_normed, d_normed[::-1]).reshape(rows, feats)
    proj = jnp.sum(d_normed * gain[None, :] * values, axis=1).reshape(1, rows)
    grad_gain = jnp.sum(d_normed * values * rstd[:, None], axis=0).reshape(1, feats)
    proj, grad_gain = phase(proj, grad_gain)

    proj = proj + col_to(proj, "proj", dc=1)
    proj, grad_gain = phase(proj, grad_gain)
    proj = proj + col_to(proj, "proj", dx=1)
    grad_gain = grad_gain + row_to(grad_gain, "gain", dl=1)
    proj, grad_gain, hid_b = phase(proj, grad_gain, hid_b)
    hid_b_other = col_to(hid_b, "hid_core", dc=1)
    proj = proj + neighbour(proj, "proj")
    grad_gain = grad_gain + neighbour_row(grad_gain, "gain")
    proj, grad_gain, hid_b, hid_b_other = phase(proj, grad_gain, hid_b, hid_b_other)
    grad_gain = grad_gain + row_to(grad_gain, "gain", dy=2)
    grad_down = down_grads(hid_b, hid_b_other, out_down, width, 1, down_a, 3)
    proj = (proj + col_to(proj, "proj", dz=2)).reshape(rows)
    scaled = rstd * rstd * rstd * proj / total_feats
    d_input = (
        out_grad.astype(F32) + rstd[:, None] * d_normed * gain[None, :] - values * scaled[:, None]
    ).astype(BF16)
    return (d_input, grad_gain.reshape(feats), grad_gate, grad_up, grad_down)


def solution(mesh):
    in_specs = (
        P("row", "col"),
        P("row", "col"),
        P("col"),
        P("col", "row"),
        P("col", "row"),
        P("row", "col"),
        P("col", "row"),
        P("col", "row"),
    )
    out_specs = (P("row", "col"), P("col"), P("col", "row"), P("col", "row"), P("row", "col"))
    return jax.shard_map(local, mesh=mesh, in_specs=in_specs, out_specs=out_specs, check_vma=False)
```

```python
import jax
import jax.numpy as jnp
from jax import lax
from jax.experimental import pallas as pl
from jax.experimental.pallas import tpu as pltpu
from jax.sharding import PartitionSpec as P

EPS = 1e-05
NZ, NX, NC = 4, 2, 2
NY, NL = 4, 2
F32, BF16 = jnp.float32, jnp.bfloat16


def dot(left, right, a, b):
    return lax.dot_general(left, right, (((a,), (b,)), ((), ())), preferred_element_type=F32)


def kernel_call(body, name, steps, in_specs, out_specs, out_shape, scratch, args):
    return pl.pallas_call(
        body,
        grid=(steps,),
        in_specs=in_specs,
        out_specs=out_specs,
        out_shape=out_shape,
        scratch_shapes=scratch,
        compiler_params=pltpu.CompilerParams(vmem_limit_bytes=60 * 2**20),
        name=name,
    )(*args)


def hidden_units(left, left_other, w, w_other, part, kinds, steps):
    f, (width, m) = left.shape[1], (w.shape[0], left.shape[0] // NX)
    n, tok = width // steps, m // len(kinds)

    def body(l, lo, w, wo, *outs):
        total = dot(l[...], w[...], 1, 1) + dot(lo[...], wo[...], 1, 1)
        for at, out in enumerate(outs):
            out[...] = total[at * tok:(at + 1) * tok].astype(out.dtype)

    lefts = [pl.BlockSpec((m, f), lambda i: (part, 0))] * 2
    rights = [pl.BlockSpec((n, f), lambda i: (i, 0))] * 2
    return kernel_call(
        body, "hidden_units", steps, lefts + rights, [pl.BlockSpec((tok, n), lambda i: (0, i))] * len(kinds),
        [jax.ShapeDtypeStruct((tok, width), kind) for kind in kinds], [], (left, left_other, w, w_other),
    )


def at_block(rows, n, block):
    return pl.BlockSpec((rows, n), lambda i: (block, i))


def input_grads(gate, up, w_gate, w_up, tok, steps):
    f, width = w_gate.shape
    k, count = width // steps, len(gate)

    def body(*refs):
        gates, ups, (wg, wu, out) = refs[:count], refs[count:2 * count], refs[2 * count:]
        total = dot(jnp.concatenate([p[...] for p in gates], axis=0), wg[...], 1, 1)
        total += dot(jnp.concatenate([p[...] for p in ups], axis=0), wu[...], 1, 1)

        @pl.when(pl.program_id(0) == 0)
        def _():
            out[...] = total

        @pl.when(pl.program_id(0) > 0)
        def _():
            out[...] += total

    specs = [at_block(tok, k, block) for _, block in gate + up] + [at_block(f, k, 0)] * 2
    m = tok * count
    return kernel_call(
        body, "input_grads", steps, specs, pl.BlockSpec((m, f), lambda i: (0, 0)),
        jax.ShapeDtypeStruct((m, f), F32), [], (*[x for x, _ in gate + up], w_gate, w_up),
    )


def gate_up_grads(normed_t, gate, up, tok, steps):
    f, t = normed_t.shape
    width, count = gate[0][0].shape[1], len(gate)
    n = width // steps

    def body(left, *refs):
        gates, ups, (gate_out, up_out) = refs[:count], refs[count:2 * count], refs[2 * count:]
        left = left[...]
        gate_out[...] = dot(left, jnp.concatenate([p[...] for p in gates], axis=0), 1, 0).astype(BF16)
        up_out[...] = dot(left, jnp.concatenate([p[...] for p in ups], axis=0), 1, 0).astype(BF16)

    specs = [pl.BlockSpec((f, t), lambda i: (0, 0))] + [at_block(tok, n, block) for _, block in gate + up]
    return kernel_call(
        body, "gate_up_grads", steps, specs, [at_block(f, n, 0)] * 2,
        [jax.ShapeDtypeStruct((f, width), BF16)] * 2, [], (normed_t, *[x for x, _ in gate + up]),
    )


def down_grads(hid, hid_other, out, width, first, earlier, steps):
    f, (t, some) = out.shape[1], hid.shape
    n = some // steps

    def body(left, left_other, right, *refs):
        refs[-1][...] = (dot(left[...], right[:t], 0, 0) + dot(left_other[...], right[t:], 0, 0)).astype(BF16)

    specs = [at_block(t, n, 0)] * 2 + [pl.BlockSpec((2 * t, f), lambda i: (0, 0))]
    more = () if earlier is None else (earlier,)
    return pl.pallas_call(
        body,
        grid=(steps,),
        in_specs=specs + [pl.BlockSpec(memory_space=pl.ANY)] * len(more),
        out_specs=pl.BlockSpec((n, f), lambda i: (first + i, 0)),
        out_shape=jax.ShapeDtypeStruct((width, f), BF16),
        input_output_aliases={3: 0} if more else {},
        compiler_params=pltpu.CompilerParams(vmem_limit_bytes=60 * 2**20),
        name="down_grads",
    )(hid, hid_other, out, *more)


def col_to(x, name, dz=0, dx=0, dc=0):
    pairs = []
    for z in range(NZ):
        for h in range(NX):
            for c in range(NC):
                dst = (((z + dz) % NZ) * NX + (h + dx) % NX) * NC + (c + dc) % NC
                pairs.append(((z * NX + h) * NC + c, dst))
    with jax.named_scope(name):
        return lax.ppermute(x, "col", pairs)


def row_to(x, name, dy=0, dl=0):
    pairs = []
    for y in range(NY):
        for l in range(NL):
            pairs.append((y * NL + l, ((y + dy) % NY) * NL + (l + dl) % NL))
    with jax.named_scope(name):
        return lax.ppermute(x, "row", pairs)


def phase(*arrays):
    return lax.optimization_barrier(arrays)


def local(inputs, out_grad, gain, w_gate, w_up, w_down, gate_pre, up_pre):
    rows, feats = inputs.shape
    width = gate_pre.shape[1]
    tok = gate_pre.shape[0]
    half = tok // 2
    total_feats = feats * NZ * NX * NC
    steps = 2 if width % 256 == 0 else 1
    ahead = width // 4
    col, row = lax.axis_index("col"), lax.axis_index("row")
    z, h, c = col // (NX * NC), (col // NC) % NX, col % NC
    y, l = row // NL, row % NL

    same = (l + h) % NX == 0

    def order(mine, other):
        f = mine.shape[1]
        mine, other = mine.reshape(NC, tok, f), other.reshape(NC, tok, f)
        pair = jnp.stack([jnp.where(same, mine, other), jnp.where(same, other, mine)])
        return jnp.where(c == 0, pair, pair[:, ::-1])[:, :, None]

    def assemble(pairs):
        both = [jnp.zeros((NX, NZ, *pairs[0].shape[3:]), pairs[0].dtype) for _ in range(NC)]
        for ky, pair in enumerate(pairs):
            at = (0, (y + ky - z) % NZ, 0, 0)
            both = [lax.dynamic_update_slice(full, pair[:, i], at) for i, full in enumerate(both)]
        return [full.reshape(-1, full.shape[3]) for full in both]

    def neighbour(x, name):
        with jax.named_scope(name):
            return lax.ppermute(x, "col", [(i, i ^ NC * NX) for i in range(NZ * NX * NC)])

    def neighbour_row(x, name):
        with jax.named_scope(name):
            return lax.ppermute(x, "row", [(i, i ^ NL) for i in range(NY * NL)])

    def gather_hidden(x, name):
        groups = [[chip * NC + core for chip in range(NZ * NX)] for core in range(NC)]
        copies = x if x.ndim == 3 else jnp.broadcast_to(x[None], (NZ * NX, *x.shape))
        with jax.named_scope(name):
            return lax.all_to_all(copies, "col", 0, 0, axis_index_groups=groups, tiled=True).reshape(-1, x.shape[-1])

    out_xl = row_to(out_grad, "out_xl", dl=1)
    w_down_other = col_to(w_down, "w_down", dc=1)
    gates = gate_pre.astype(F32)
    ups = up_pre.astype(F32)
    sig = jax.nn.sigmoid(gates)
    hidden = (gates * sig * ups).astype(BF16)
    hidden_a, hidden_b = hidden[:, :ahead], hidden[:, ahead:]
    values = inputs.astype(F32)
    squares = jnp.sum(values * values, axis=1).reshape(1, rows)
    squares = squares + col_to(squares, "squares", dc=1)
    pair = order(out_grad, out_xl)
    hidden_a = jnp.broadcast_to(hidden_a[None], (NZ * NX, *hidden_a.shape))
    pair, hidden_a, hidden_b, w_down_other, squares = phase(pair, hidden_a, hidden_b, w_down_other, squares)

    out_y = [row_to(pair, "out_y", -ky) for ky in range(1, NY)]
    hid_a = gather_hidden(hidden_a, "hid_a")
    squares = squares + neighbour(squares, "squares")
    out_mine, out_theirs = assemble([pair] + out_y)
    hid_copies = jnp.broadcast_to(hidden_b[None], (NZ * NX, *hidden_b.shape))
    out_mine, out_theirs, squares, hid_copies = phase(out_mine, out_theirs, squares, hid_copies)

    out_other = col_to(out_theirs, "out_core", dc=1)
    far0, far1, far2, far3 = hidden_units(
        out_mine, out_other, w_down, w_down_other, 1, (F32, BF16, BF16, BF16), steps
    )
    far0, far1, far2, far3, out_mine, out_other, hid_a, squares = phase(
        far0, far1, far2, far3, out_mine, out_other, hid_a, squares
    )

    x_in = col_to(far2, "rs_x", dx=1)
    b_in = col_to(far1, "rs_b", dz=1)
    a_in = col_to(far3, "rs_a", dz=-1)
    near0, near1, near2, near3 = hidden_units(out_mine, out_other, w_down, w_down_other, 0, (F32,) * NZ, steps)
    squares = phase(squares, near0)[0]
    squares = squares + col_to(squares, "squares", dz=2)
    x_in, b_in, a_in, near0, near1, near2, near3, squares, hid_a = phase(
        x_in, b_in, a_in, near0, near1, near2, near3, squares, hid_a
    )
    b_half = col_to((near2[:half] + x_in[:half].astype(F32)).astype(BF16), "rs_fb", dz=1)
    a_half = col_to((near2[half:] + x_in[half:].astype(F32)).astype(BF16), "rs_fa", dz=-1)
    x_last = col_to((far0 + b_in.astype(F32) + a_in.astype(F32)).astype(BF16), "rs_xl", dx=1)
    b_sum = jnp.concatenate([near1[:half] + b_half.astype(F32), near1[half:]], axis=0).astype(BF16)
    a_sum = jnp.concatenate([near3[:half], near3[half:] + a_half.astype(F32)], axis=0).astype(BF16)
    b_sum, a_sum, out_mine, out_theirs, squares, hid_a = phase(b_sum, a_sum, out_mine, out_theirs, squares, hid_a)
    b_last = col_to(b_sum, "rs_bl", dz=1)
    a_last = col_to(a_sum, "rs_al", dz=-1)
    squares = squares + col_to(squares, "squares", dx=1)
    rstd = lax.rsqrt(squares.reshape(rows) / total_feats + EPS)
    normed = (values * rstd[:, None] * gain[None, :]).astype(BF16)
    copies = jnp.broadcast_to(normed[None], (NY * NL, rows, feats))
    with jax.named_scope("normed_rows"):
        whole = lax.all_to_all(copies, "row", 0, 0, tiled=True)
    d_hidden = near0 + x_last.astype(F32) + b_last.astype(F32) + a_last.astype(F32)
    silu = gates * sig
    d_gate = (d_hidden * ups * sig * (1.0 + gates * (1.0 - sig))).astype(BF16)
    d_up = (d_hidden * silu).astype(BF16)
    both = jnp.concatenate([d_gate, d_up], axis=0)
    d_gate, d_up, both, hid_a, rstd, out_mine, out_theirs = phase(
        d_gate, d_up, both, hid_a, rstd, out_mine, out_theirs
    )

    gate_b = col_to(d_gate, "ag_gate_b", dz=1)
    up_a = col_to(d_up, "ag_up_a", dz=-1)
    up_b = col_to(d_up, "ag_up_b", dz=1)
    gate_a = col_to(d_gate, "ag_gate_a", dz=-1)
    both_x = col_to(both, "ag_x", dx=1)
    def by_chip(x):
        x = x.reshape(NX, NZ, tok, feats)
        x = jnp.where(h == 0, x, x[::-1]).transpose(1, 0, 2, 3)
        return lax.dynamic_slice_in_dim(jnp.concatenate([x, x]), (NZ - z) % NZ, NZ).reshape(-1, feats)

    out_down = jnp.concatenate([by_chip(out_mine), by_chip(out_theirs)], axis=0)
    pairs = []
    for at in range(NY):
        even, odd = whole[at * NL].reshape(NC, tok, feats), whole[at * NL + 1].reshape(NC, tok, feats)
        one = jnp.stack([jnp.where(h == 0, even, odd), jnp.where(h == 0, odd, even)])
        pairs.append(jnp.where(c == 0, one, one[:, ::-1])[:, :, None])
    normed_all = jnp.zeros((NX, NC, NZ, tok, feats), BF16)
    for at, one in enumerate(pairs):
        normed_all = lax.dynamic_update_slice(normed_all, one, (0, 0, (at - z) % NZ, 0, 0))
    normed_t = normed_all.reshape(-1, feats).T
    swapped = [col_to(piece, "ag_core", dc=1) for piece in (up_a, gate_a, gate_b, up_b)]
    gate_b, up_a, up_b, gate_a, both_x, both, hid_a, normed_t, out_down, *swapped = phase(
        gate_b, up_a, up_b, gate_a, both_x, both, hid_a, normed_t, out_down, *swapped
    )

    gate_f = col_to(gate_b, "ag_gate_f", dz=1)
    up_f = col_to(up_a, "ag_up_f", dz=-1)
    hid_a_other = col_to(hid_a, "hid_core", dc=1)
    swapped = [col_to(both, "ag_core", dc=1), *swapped, col_to(both_x, "ag_core", dc=1)]
    gate_f, up_f, both, gate_b, up_a, up_b, gate_a, both_x, normed_t, hid_a, hid_a_other, *swapped = phase(
        gate_f, up_f, both, gate_b, up_a, up_b, gate_a, both_x, normed_t, hid_a, hid_a_other, *swapped
    )

    both_xb = col_to(both_x, "ag_xb", dz=1)
    both_xa = col_to(both_x, "ag_xa", dz=-1)
    gate_xf = col_to(gate_f, "ag_gate_xf", dx=1)
    up_xf = col_to(up_f, "ag_up_xf", dx=1)
    swapped_f = [col_to(piece, "ag_core", dc=1) for piece in (gate_f, up_f)]

    near_ones = [both, up_a, gate_a, gate_f, up_f, gate_b, up_b, both_x]
    swapped = swapped[:3] + swapped_f + swapped[3:]

    def by_k(both, up_a, gate_a, gate_f, up_f, gate_b, up_b, both_x):
        gate = [(both, 0), (gate_a, 0), (gate_f, 0), (gate_b, 0)]
        up = [(both, 1), (up_a, 0), (up_f, 0), (up_b, 0)]
        return gate, up, [(both_x, 0)], [(both_x, 1)]

    gate_mine, up_mine, gate_x, up_x = by_k(*near_ones)
    gate_theirs, up_theirs, gate_xt, up_xt = by_k(*swapped)
    gate_first = gate_mine + gate_theirs + gate_x + gate_xt
    up_first = up_mine + up_theirs + up_x + up_xt
    term_first = input_grads(gate_first, up_first, w_gate, w_up, tok, steps)

    term_first, hid_a = phase(term_first, hid_a)
    down_a = down_grads(hid_a, hid_a_other, out_down, width, 0, None, 1)
    both_xb, both_xa, gate_xf, up_xf, term_first, hid_copies, down_a = phase(
        both_xb, both_xa, gate_xf, up_xf, term_first, hid_copies, down_a
    )
    hid_b = gather_hidden(hid_copies, "hid_b")

    far_ones = [both_xa, gate_xf, up_xf, both_xb]
    swapped_far = [col_to(piece, "ag_core", dc=1) for piece in far_ones]

    def by_k_far(both_xa, gate_xf, up_xf, both_xb):
        return [(both_xa, 0), (gate_xf, 0), (both_xb, 0)], [(both_xa, 1), (up_xf, 0), (both_xb, 1)]

    gate_xmine, up_xmine = by_k_far(*far_ones)
    gate_xtheirs, up_xtheirs = by_k_far(*swapped_far)
    term_second = input_grads(gate_xmine + gate_xtheirs, up_xmine + up_xtheirs, w_gate, w_up, tok, steps)
    gate_all = gate_mine + gate_theirs + gate_x + gate_xmine + gate_xt + gate_xtheirs
    up_all = up_mine + up_theirs + up_x + up_xmine + up_xt + up_xtheirs
    term = jnp.concatenate([
        term_first[:9 * tok], term_second[:3 * tok], term_first[9 * tok:], term_second[3 * tok:]
    ], axis=0).reshape(NX, NC, NZ, tok, feats)
    def term_of(ky):
        return lax.dynamic_slice(term, (0, 0, (y + ky - z) % NZ, 0, 0), (NX, NC, 1, tok, feats))[:, :, 0]

    mine, normed_t, *sent = phase(term_of(0), normed_t, *[term_of(ky).astype(BF16) for ky in range(1, NY)])
    received = [row_to(piece, "dn_y", ky + 1) for ky, piece in enumerate(sent)]
    grad_gate, grad_up = gate_up_grads(normed_t, gate_all, up_all, tok, steps)
    d_normed = mine
    for piece in received:
        d_normed = d_normed + piece.astype(F32)
    near, far = (jnp.where(same, d_normed[i], d_normed[1 - i]) for i in range(2))
    near, far, grad_gate, grad_up = phase(near, far.astype(BF16), grad_gate, grad_up)

    d_normed = near + row_to(far, "dn_xl", dl=1).astype(F32)
    d_normed = jnp.where(c == 0, d_normed, d_normed[::-1]).reshape(rows, feats)
    proj = jnp.sum(d_normed * gain[None, :] * values, axis=1).reshape(1, rows)
    grad_gain = jnp.sum(d_normed * values * rstd[:, None], axis=0).reshape(1, feats)
    proj, grad_gain = phase(proj, grad_gain)

    proj = proj + col_to(proj, "proj", dc=1)
    proj, grad_gain = phase(proj, grad_gain)
    proj = proj + col_to(proj, "proj", dx=1)
    grad_gain = grad_gain + row_to(grad_gain, "gain", dl=1)
    proj, grad_gain, hid_b = phase(proj, grad_gain, hid_b)
    hid_b_other = col_to(hid_b, "hid_core", dc=1)
    proj = proj + neighbour(proj, "proj")
    grad_gain = grad_gain + neighbour_row(grad_gain, "gain")
    proj, grad_gain, hid_b, hid_b_other = phase(proj, grad_gain, hid_b, hid_b_other)
    grad_gain = grad_gain + row_to(grad_gain, "gain", dy=2)
    grad_down = down_grads(hid_b, hid_b_other, out_down, width, 1, down_a, 3)
    proj = (proj + col_to(proj, "proj", dz=2)).reshape(rows)
    scaled = rstd * rstd * rstd * proj / total_feats
    d_input = (
        out_grad.astype(F32) + rstd[:, None] * d_normed * gain[None, :] - values * scaled[:, None]
    ).astype(BF16)
    return (d_input, grad_gain.reshape(feats), grad_gate, grad_up, grad_down)


def solution(mesh):
    in_specs = (
        P("row", "col"),
        P("row", "col"),
        P("col"),
        P("col", "row"),
        P("col", "row"),
        P("row", "col"),
        P("col", "row"),
        P("col", "row"),
    )
    out_specs = (P("row", "col"), P("col"), P("col", "row"), P("col", "row"), P("row", "col"))
    return jax.shard_map(local, mesh=mesh, in_specs=in_specs, out_specs=out_specs, check_vma=False)
```
